256 devices in a mesh: fsdp: 16 (over x, y), tp: 16 (over z, core).
Axes of the slice: x: 4, y: 4, z: 8, core: 2. Of those that a mesh axis runs over, the one named last changes fastest.
Arguments:
- momentum: bfloat16 [8192, 26624], P('fsdp', 'tp'), may hold values from -6 to 6
- gradient: bfloat16 [8192, 26624], P('fsdp', 'tp'), may hold values from -3 to 3
- basis: bfloat16 [26624, 256], P('tp'), may hold values from -0.010663815 to 0.010663815
Outputs:
- momentum_next: bfloat16 [8192, 26624], P('fsdp', 'tp')
- basis_next: bfloat16 [26624, 256], P('tp')
- update: bfloat16 [8192, 26624], P('fsdp', 'tp')
The draws below stay inside these ranges and needn't reach their ends.
All inputs are finite; a program needn't handle non-finite values.
Results may differ from the reference program's by a relative error of at most 0.009.
Values may be sent and summed in bfloat16 or wider, within the bound.
No kernel may reach another device: no remote copies, remote signals or barrier semaphores. Data moves between devices by JAX's collectives and lax.ppermute only.
A program may use at most 64 MiB of HBM per device.

```python
import jax
import jax.numpy as jnp
from jax import lax

M_ROWS = 8192
N_COLS = 26624
RANK = 256


def shared_columns(key):
    return jax.random.randint(jax.random.fold_in(key, 77), (N_COLS, RANK), -255, 256, dtype=jnp.int32).astype(jnp.float32)


def rising_scale(low_end, high_end):
    position = jnp.arange(N_COLS, dtype=jnp.float32) / max(N_COLS - 1, 1)
    return jnp.exp(jnp.log(low_end) + position * (jnp.log(high_end) - jnp.log(low_end)))


def draw_basis(key, part):
    columns = shared_columns(key)
    key = jax.random.fold_in(key, 3)
    col_signs = (2 * jax.random.randint(key, (1, RANK), 0, 2, dtype=jnp.int32) - 1).astype(jnp.float32)
    spread = (255.0 * 256.0 / 3.0) ** 0.5
    return (columns * col_signs * (1.0 / (spread * N_COLS ** 0.5))).astype(jnp.bfloat16)


def draw_momentum(key, part):
    columns = shared_columns(key)
    key = jax.random.fold_in(key, 5)
    coeff_key, noise_key = jax.random.split(key, 2)
    levels = jnp.arange(RANK, dtype=jnp.int32)
    top_level = 5 + 10 * (RANK - 1 - levels) // max(RANK - 1, 1)
    coeffs = jax.random.randint(coeff_key, (M_ROWS, RANK), -top_level[None, :], top_level[None, :] + 1, dtype=jnp.int32).astype(jnp.float32)
    planted = jnp.dot(coeffs, columns.T, precision=lax.Precision.HIGHEST, preferred_element_type=jnp.float32)
    amplitude_sum = jnp.sum(top_level * (top_level + 1)).astype(jnp.float32)
    variance = 255.0 * 256.0 / 3.0 * amplitude_sum / 3.0
    planted = planted * (1.2 / jnp.sqrt(variance))
    planted = planted * rising_scale(0.6, 2.0)[None, :]
    noise_part = 0.5 * jax.random.normal(noise_key, (M_ROWS, N_COLS), jnp.float32)
    return jnp.clip(planted + noise_part, -6.0, 6.0).astype(jnp.bfloat16)


def level_of(rng, dims, cuts, smallest, high):
    level, own = 1.0, jax.random.fold_in(rng, 6)
    for axis_at, blocks in cuts:
        steps = jnp.exp(jax.random.uniform(jax.random.fold_in(own, axis_at), (blocks,), jnp.float32, smallest / len(cuts), high / len(cuts)))
        level = level * jnp.repeat(steps, dims[axis_at] // blocks).reshape([-1 if axis == axis_at else 1 for axis in range(len(dims))])
    return level


def scatter_about(key, extent, scale, reach, cuts=(), held_as=jnp.bfloat16):
    level = level_of(key, extent, cuts, -0.22, 0.18) if cuts else 1.0
    values = jax.random.normal(key, extent, jnp.float32) * scale * level
    return jnp.minimum(jnp.maximum(values, -reach), reach).astype(held_as)


def setup_inputs(seed: int = 0) -> dict:
    arg_keys = jax.random.split(jax.random.key(seed), 4)
    return {
        "momentum": draw_momentum(jax.random.fold_in(arg_keys[3], 71), 0),
        "gradient": scatter_about(arg_keys[1], (M_ROWS, N_COLS), 0.5, 3.0, ((0, 16), (1, 16))),
        "basis": draw_basis(jax.random.fold_in(arg_keys[3], 71), 0),
    }


def reference(momentum, gradient, basis):
    blended = (momentum.astype(jnp.float32) + gradient.astype(jnp.float32)).astype(jnp.bfloat16)
    left = jnp.dot(blended.astype(jnp.float32), basis.astype(jnp.float32), preferred_element_type=jnp.float32)
    gram = jnp.dot(left.T.astype(jnp.float32), left.astype(jnp.float32), precision=lax.Precision.HIGHEST, preferred_element_type=jnp.float32)
    gram = gram + 0.001 * jnp.eye(RANK, dtype=jnp.float32)
    factor = jnp.linalg.cholesky(gram)
    ortho = lax.linalg.triangular_solve(factor, left, left_side=False, lower=True, transpose_a=True).astype(jnp.bfloat16)
    right = lax.dot_general(blended.astype(jnp.float32), ortho.astype(jnp.float32), (((0,), (0,)), ((), ())), preferred_element_type=jnp.float32)
    colsq = lax.optimization_barrier(jnp.sum(right * right, axis=0))
    basis_next = (right * lax.rsqrt(colsq + 1e-06)).astype(jnp.bfloat16)
    right_low = right.astype(jnp.bfloat16)
    feedback = lax.dot_general(ortho.astype(jnp.float32), right_low.astype(jnp.float32), (((1,), (1,)), ((), ())), preferred_element_type=jnp.float32)
    momentum_next = (blended.astype(jnp.float32) - 0.1 * feedback).astype(jnp.bfloat16)
    scale = math_scale()
    product = lax.dot_general(ortho.astype(jnp.float32), basis_next.astype(jnp.float32), (((1,), (1,)), ((), ())), preferred_element_type=jnp.float32)
    update = (scale * product).astype(jnp.bfloat16)
    return (momentum_next, basis_next, update)

def math_scale():
    return (M_ROWS * N_COLS / RANK) ** 0.5
```

```python
import functools

import jax
import jax.numpy as jnp
from jax import lax
from jax.experimental import pallas as pl
from jax.experimental.pallas import tpu as pltpu
from jax.sharding import PartitionSpec as P

M_ROWS = 8192
N_COLS = 26624
RANK = 256
SCALE = (M_ROWS * N_COLS / RANK) ** 0.5
EXACT = lax.Precision.HIGHEST
F32, BF16 = jnp.float32, jnp.bfloat16
PANEL = 32
VMEM = pl.BlockSpec(memory_space=pltpu.VMEM)
SMEM = pl.BlockSpec(memory_space=pltpu.SMEM)


def iota(shape, dim):
    return lax.broadcasted_iota(jnp.int32, shape, dim)


def call(body, out, n_in, name, scalars=0, scratch=(), limit=48 << 20):
    many = isinstance(out, (list, tuple))
    return pl.pallas_call(
        body,
        out_shape=out,
        in_specs=[SMEM] * scalars + [VMEM] * n_in,
        out_specs=[VMEM] * len(out) if many else VMEM,
        scratch_shapes=list(scratch),
        compiler_params=pltpu.CompilerParams(vmem_limit_bytes=limit),
        name=name,
    )


def shape(dims, dtype=F32):
    return jax.ShapeDtypeStruct(dims, dtype)


def blend_body(core_ref, momentum_ref, gradient_ref, basis_ref, blended_ref, keep_ref, send_ref):
    step = pl.program_id(0)
    blended = (momentum_ref[...].astype(F32) + gradient_ref[...].astype(F32)).astype(BF16)
    blended_ref[...] = blended
    left = jnp.dot(blended, basis_ref[...], preferred_element_type=F32)
    rows = left.shape[0]
    half = keep_ref.shape[0]
    at = pl.ds(pl.multiple_of((step * rows) % half, rows), rows)
    mine = (step * rows) // half == core_ref[0]

    @pl.when(mine)
    def _():
        keep_ref[at, :] = left

    @pl.when(jnp.logical_not(mine))
    def _():
        send_ref[at, :] = left


def blend(core, momentum, gradient, basis):
    rows, cols = momentum.shape
    rank = basis.shape[1]
    block = rows // 4
    tile = pl.BlockSpec((block, cols), lambda i, c: (i, 0))
    held = pl.BlockSpec((rows // 2, rank), lambda i, c: (0, 0))
    return pl.pallas_call(
        blend_body,
        grid_spec=pltpu.PrefetchScalarGridSpec(
            num_scalar_prefetch=1,
            grid=(4,),
            in_specs=[tile, tile, pl.BlockSpec((cols, rank), lambda i, c: (0, 0))],
            out_specs=[tile, held, held],
        ),
        out_shape=[shape((rows, cols), BF16), shape((rows // 2, rank)), shape((rows // 2, rank))],
        compiler_params=pltpu.CompilerParams(vmem_limit_bytes=48 << 20),
        name="blend",
    )(core, momentum, gradient, basis)


def sum_and_spread_body(parts_ref, out_ref):
    total = parts_ref[0]
    for i in range(1, parts_ref.shape[0]):
        total = total + parts_ref[i]
    for i in range(out_ref.shape[0]):
        out_ref[i] = total


def sum_and_spread(parts, name):
    return call(sum_and_spread_body, shape(parts.shape), 1, name)(parts)


def gram_body(mine_ref, other_ref, gram_ref):
    both = (((0,), (0,)), ((), ()))
    a, b = mine_ref[...], other_ref[...]
    gram_ref[...] = lax.dot_general(a, a, both, precision=EXACT, preferred_element_type=F32) + lax.dot_general(
        b, b, both, precision=EXACT, preferred_element_type=F32
    )


def split(value):
    high = value.astype(BF16)
    rest = value - high.astype(F32)
    mid = rest.astype(BF16)
    return high, mid, (rest - mid.astype(F32)).astype(BF16)


def project_body(core_ref, blended_ref, mine_ref, other_ref, out_ref):
    half = mine_ref.shape[0]
    core = core_ref[0]
    rows = (((0,), (0,)), ((), ()))
    first = pl.ds(pl.multiple_of(core * half, half), half)
    second = pl.ds(pl.multiple_of((1 - core) * half, half), half)
    rank = out_ref.shape[1]
    total = None
    for at, ref in ((first, mine_ref), (second, other_ref)):
        parts = jnp.concatenate(split(ref[...]), axis=1)
        part = lax.dot_general(blended_ref[at, :], parts, rows, preferred_element_type=F32)
        part = part[:, :rank] + (part[:, rank : 2 * rank] + part[:, 2 * rank :])
        total = part if total is None else total + part
    out_ref[...] = total


def diag_inverse(block):
    b = block.shape[0]
    rows = iota((b, 1), 0)
    eye = rows == iota((b, b), 1)
    aug = jnp.concatenate([block, jnp.where(eye, 1.0, 0.0)], axis=1)
    for j in range(b):
        factor = jnp.where(rows > j, aug[:, j : j + 1] * (1.0 / aug[j : j + 1, j : j + 1]), 0.0)
        aug = aug - factor * aug[j : j + 1, :]
    diag = jnp.sum(jnp.where(eye, aug[:, :b], 0.0), axis=1, keepdims=True)
    return aug[:, b:] * lax.rsqrt(diag)


def inverse_factor_body(gram_ref, inv_ref, work_ref):
    rank = gram_ref.shape[0]
    eye = iota((rank, rank), 0) == iota((rank, rank), 1)
    work_ref[:, :rank] = gram_ref[...] + jnp.where(eye, 0.001, 0.0)
    work_ref[:, rank:] = jnp.where(eye, 1.0, 0.0)
    for p in range(0, rank, PANEL):
        q = p + PANEL
        inverse = diag_inverse(work_ref[p:q, p:q])
        panel = jnp.dot(inverse, work_ref[p:q, :], precision=EXACT, preferred_element_type=F32)
        work_ref[p:q, :] = panel
        if q < rank:
            work_ref[q:, :] -= lax.dot_general(
                panel[:, q:rank], panel, (((0,), (0,)), ((), ())), precision=EXACT, preferred_element_type=F32
            )
    inv_ref[...] = work_ref[:, rank:]


def times_transposed(a, b):
    return lax.dot_general(a, b, (((1,), (1,)), ((), ())), precision=EXACT, preferred_element_type=F32)


def right_body(parts_ref, inv_ref, low_ref, colsq_ref):
    total = parts_ref[0]
    for i in range(1, parts_ref.shape[0]):
        total = total + parts_ref[i]
    right = times_transposed(total, inv_ref[...])
    low = right.astype(BF16)
    for i in range(low_ref.shape[0]):
        low_ref[i] = low
    colsq_ref[...] = jnp.broadcast_to(jnp.sum(right * right, axis=0, keepdims=True), colsq_ref.shape)


def ortho_body(core_ref, mine_ref, other_ref, inv_ref, ortho_ref):
    half = mine_ref.shape[0]
    core = core_ref[0]
    inverse = inv_ref[...]
    ortho_ref[pl.ds(pl.multiple_of(core * half, half), half), :] = times_transposed(mine_ref[...], inverse).astype(BF16)
    ortho_ref[pl.ds(pl.multiple_of((1 - core) * half, half), half), :] = times_transposed(
        other_ref[...], inverse
    ).astype(BF16)


def finish_body(blended_ref, ortho_ref, right_ref, colsq_ref, momentum_ref, update_ref, basis_ref):
    @pl.when(pl.program_id(0) == 0)
    def _():
        colsq = jnp.sum(colsq_ref[...], axis=0, keepdims=True)
        basis_ref[...] = (right_ref[...].astype(F32) * lax.rsqrt(colsq + 1e-06)).astype(BF16)

    ortho = ortho_ref[...]
    across = (((1,), (1,)), ((), ()))
    feedback = lax.dot_general(ortho, right_ref[...], across, preferred_element_type=F32)
    momentum_ref[...] = (blended_ref[...].astype(F32) - 0.1 * feedback).astype(BF16)
    product = lax.dot_general(ortho, basis_ref[...], across, preferred_element_type=F32)
    update_ref[...] = (SCALE * product).astype(BF16)


def finish(blended, ortho, right, colsq):
    rows, cols = blended.shape
    rank = ortho.shape[1]
    steps = 4
    block = rows // steps
    tile = pl.BlockSpec((block, cols), lambda i: (i, 0))
    return pl.pallas_call(
        finish_body,
        grid=(steps,),
        in_specs=[
            tile,
            pl.BlockSpec((block, rank), lambda i: (i, 0)),
            pl.BlockSpec((cols, rank), lambda i: (0, 0)),
            pl.BlockSpec(colsq.shape, lambda i: (0, 0)),
        ],
        out_specs=[tile, tile, pl.BlockSpec((cols, rank), lambda i: (0, 0))],
        out_shape=[shape((rows, cols), BF16), shape((rows, cols), BF16), shape((cols, rank), BF16)],
        compiler_params=pltpu.CompilerParams(vmem_limit_bytes=48 << 20),
        name="finish",
    )(blended, ortho, right, colsq)


def on_device(momentum, gradient, basis, n_fsdp, n_tp):
    rank = basis.shape[1]
    rows, cols = momentum.shape
    chips = n_tp // 2
    pairs = [(i, i ^ 1) for i in range(n_tp)]
    along_z = [[2 * z + c for z in range(chips)] for c in range(2)]
    core = (lax.axis_index("tp") % 2).astype(jnp.int32)[None]

    blended, keep, send = blend(core, momentum, gradient, basis)
    half = keep + lax.ppermute(send, "tp", pairs)
    parts = lax.all_to_all(half.reshape(chips, -1, rank), "tp", 0, 0, axis_index_groups=along_z, tiled=True)
    spread = sum_and_spread(parts, "left_sum")
    mine = lax.all_to_all(spread, "tp", 0, 0, axis_index_groups=along_z, tiled=True).reshape(rows // 2, rank)
    other = lax.ppermute(mine, "tp", pairs)

    gram = call(gram_body, shape((rank, rank)), 2, "gram")(mine, other)
    gram_parts = lax.all_to_all(gram.reshape(n_fsdp, -1, rank), "fsdp", 0, 0, tiled=True)
    project = call(project_body, shape((cols, rank)), 3, "project", scalars=1)(core, blended, mine, other)
    project_parts = lax.all_to_all(project.reshape(n_fsdp, -1, rank), "fsdp", 0, 0, tiled=True)
    gram = lax.all_to_all(sum_and_spread(gram_parts, "gram_sum"), "fsdp", 0, 0, tiled=True).reshape(rank, rank)
    inverse = call(
        inverse_factor_body, shape((rank, rank)), 1, "inverse_factor", scratch=[pltpu.VMEM((rank, 2 * rank), F32)]
    )(gram)

    low, colsq = call(right_body, [shape(project_parts.shape, BF16), shape((n_fsdp * n_tp, rank))], 2, "right")(
        project_parts, inverse
    )
    right = lax.all_to_all(low, "fsdp", 0, 0, tiled=True).reshape(cols, rank)
    colsq = lax.all_to_all(colsq, ("fsdp", "tp"), 0, 0, tiled=True)
    ortho = call(ortho_body, shape((rows, rank), BF16), 3, "ortho", scalars=1)(core, mine, other, inverse)
    momentum_next, update, basis_next = finish(blended, ortho, right, colsq)
    return momentum_next, basis_next, update


def solution(mesh):
    body = functools.partial(on_device, n_fsdp=mesh.shape["fsdp"], n_tp=mesh.shape["tp"])
    return jax.shard_map(
        body,
        mesh=mesh,
        in_specs=(P("fsdp", "tp"), P("fsdp", "tp"), P("tp", None)),
        out_specs=(P("fsdp", "tp"), P("tp", None), P("fsdp", "tp")),
        check_vma=False,
    )
```

```python
import functools

import jax
import jax.numpy as jnp
from jax import lax
from jax.experimental import pallas as pl
from jax.experimental.pallas import tpu as pltpu
from jax.sharding import PartitionSpec as P

M_ROWS = 8192
N_COLS = 26624
RANK = 256
SCALE = (M_ROWS * N_COLS / RANK) ** 0.5
F32, BF16 = jnp.float32, jnp.bfloat16
PANEL = 64
VMEM = pl.BlockSpec(memory_space=pltpu.VMEM)
ROWS_BY_ROWS = (((0,), (0,)), ((), ()))
COLS_BY_COLS = (((1,), (1,)), ((), ()))


def iota(shape, dim):
    return lax.broadcasted_iota(jnp.int32, shape, dim)


def shape(dims, dtype=F32):
    return jax.ShapeDtypeStruct(dims, dtype)


def call(body, out, name, *args, scratch=(), limit=24 << 20, flops=0):
    many = isinstance(out, (list, tuple))
    outs = out if many else [out]
    size = sum(a.size * a.dtype.itemsize for a in (*args, *outs))
    return pl.pallas_call(
        body,
        out_shape=out,
        in_specs=[VMEM] * len(args),
        out_specs=[VMEM] * len(outs) if many else VMEM,
        scratch_shapes=list(scratch),
        compiler_params=pltpu.CompilerParams(vmem_limit_bytes=limit),
        cost_estimate=pl.CostEstimate(flops=flops, bytes_accessed=size, transcendentals=0),
        name=name,
    )(*args)


def split(value):
    high = value.astype(BF16)
    rest = value - high.astype(F32)
    mid = rest.astype(BF16)
    return high, mid, (rest - mid.astype(F32)).astype(BF16)


def left_terms(value, axis):
    high, mid, low = split(value)
    return jnp.concatenate([high, high, mid, mid, high, low], axis=axis)


def right_terms(value):
    high, mid, low = split(value)
    return jnp.concatenate([high, mid, high, mid, low, high], axis=0)


def blend_body(momentum_ref, gradient_ref, basis_ref, blended_ref, left_ref):
    blended = (momentum_ref[...].astype(F32) + gradient_ref[...].astype(F32)).astype(BF16)
    blended_ref[...] = blended
    left_ref[...] = jnp.dot(blended, basis_ref[...], preferred_element_type=F32).astype(BF16)


def blend(momentum, gradient, basis):
    rows, cols = momentum.shape
    rank = basis.shape[1]
    steps = 4
    block = rows // steps
    tile = pl.BlockSpec((block, cols), lambda i: (i, 0))
    return pl.pallas_call(
        blend_body,
        grid=(steps,),
        in_specs=[tile, tile, pl.BlockSpec((cols, rank), lambda i: (0, 0))],
        out_specs=[tile, pl.BlockSpec((block, rank), lambda i: (i, 0))],
        out_shape=[shape((rows, cols), BF16), shape((rows, rank), BF16)],
        compiler_params=pltpu.CompilerParams(vmem_limit_bytes=58 << 20),
        name="blend",
    )(momentum, gradient, basis)


def left_sum_body(parts_ref, out_ref):
    total = parts_ref[0].astype(F32)
    for i in range(1, parts_ref.shape[0]):
        total = total + parts_ref[i].astype(F32)
    low = total.astype(BF16)
    for i in range(out_ref.shape[0]):
        out_ref[i] = low


def project_body(blended_ref, left_ref, out_ref, work_ref):
    parts = out_ref.shape[0]
    rank = left_ref.shape[1]
    some = rank // parts
    block = blended_ref.shape[1] // parts
    left = left_ref[...]
    gram = split(lax.dot_general(left, left, ROWS_BY_ROWS, preferred_element_type=F32))
    work_ref[...] = lax.dot_general(blended_ref[...], left, ROWS_BY_ROWS, preferred_element_type=F32)
    for f in range(parts):
        for i, term in enumerate(gram):
            out_ref[f, i * some : (i + 1) * some, :] = term[f * some : (f + 1) * some]
        out_ref[f, 3 * some :, :] = work_ref[f * block : (f + 1) * block, :].astype(BF16)


def project_sum_body(parts_ref, gram_ref, proj_ref):
    some = gram_ref.shape[1]
    total = parts_ref[0].astype(F32)
    for i in range(1, parts_ref.shape[0]):
        total = total + parts_ref[i].astype(F32)
    gram = (total[2 * some : 3 * some] + total[some : 2 * some]) + total[:some]
    low = total[3 * some :].astype(BF16)
    for i in range(gram_ref.shape[0]):
        gram_ref[i] = gram
        proj_ref[i] = low


def diag_inverse(block):
    b = block.shape[0]
    n, width = b // 8, 2 * b
    eye = iota((b, b), 0) == iota((b, b), 1)
    aug = jnp.concatenate([block, jnp.where(eye, 1.0, 0.0)], axis=1)
    sub = iota((8, width), 0)
    rows = [aug[8 * i : 8 * i + 8] for i in range(n)]
    for g in range(n):
        cols = [
            [jnp.broadcast_to(rows[v][:, 8 * g + k : 8 * g + k + 1], (8, width)) for v in range(g, n)] for k in range(8)
        ]
        own, pivots, scaled = rows[g], jnp.zeros((8, width), F32), []
        for m in range(8):
            pivot = jnp.broadcast_to(cols[m][0][m : m + 1], (8, width))
            pivots = jnp.where(sub == m, pivot, pivots)
            inverse = 1.0 / pivot
            scaled.append(jnp.broadcast_to(own[m : m + 1], (8, width)) * inverse)
            factor = jnp.where(sub > m, cols[m][0], 0.0)
            own = own - factor * scaled[m]
            for k in range(m + 1, 8):
                ratio = jnp.broadcast_to(cols[k][0][m : m + 1], (8, width)) * inverse
                cols[k][0] = cols[k][0] - factor * ratio
                for v in range(1, n - g):
                    cols[k][v] = cols[k][v] - cols[m][v] * ratio
        rows[g] = own * lax.rsqrt(pivots)
        for v in range(1, n - g):
            row = rows[g + v]
            for m in range(8):
                row = row - cols[m][v] * scaled[m]
            rows[g + v] = row
    return jnp.concatenate(rows, axis=0)[:, b:]


def inverse_factor_body(gram_ref, left_ref, inv_ref, ortho_ref):
    rank = gram_ref.shape[0]
    row, col = iota((rank, rank), 0), iota((rank, rank), 1)
    inv_ref[...] = gram_ref[...] + jnp.where(row == col, 0.001, 0.0)
    lanes = iota((1, rank), 1)
    for p in range(0, rank, PANEL):
        q = p + PANEL
        inverse = diag_inverse(inv_ref[p:q, p:q])
        full = jnp.dot(left_terms(inverse, 1), right_terms(inv_ref[p:q, :]), preferred_element_type=F32)
        pieces = [full[:, :p]] if p else []
        pieces.append(inverse)
        if q < rank:
            pieces.append(full[:, q:])
        panel = jnp.concatenate(pieces, axis=1)
        inv_ref[p:q, :] = panel
        if q < rank:
            change = lax.dot_general(
                left_terms(panel[:, q:], 0), right_terms(panel), ROWS_BY_ROWS, preferred_element_type=F32
            )
            inv_ref[q:, :] = jnp.where((lanes >= p) & (lanes < q), 0.0, inv_ref[q:, :]) - change
    inverse = jnp.where(row >= col, inv_ref[...], 0.0)
    inv_ref[...] = inverse
    ortho_ref[...] = by_inverse(left_ref[...], inverse).astype(BF16)


def by_inverse(low, inverse):
    n = inverse.shape[0]
    parts = lax.dot_general(low, jnp.concatenate(split(inverse), axis=0), COLS_BY_COLS, preferred_element_type=F32)
    return parts[:, :n] + (parts[:, n : 2 * n] + parts[:, 2 * n :])


def right_body(proj_ref, inv_ref, right_ref, low_ref, colsq_ref):
    right = by_inverse(proj_ref[...], inv_ref[...])
    right_ref[...] = right
    low_ref[...] = right.astype(BF16)
    colsq_ref[...] = jnp.broadcast_to(jnp.sum(right * right, axis=0)[None, None, :], colsq_ref.shape)


def feedback_body(blended_ref, ortho_ref, low_ref, momentum_ref):
    feedback = lax.dot_general(ortho_ref[...], low_ref[...], COLS_BY_COLS, preferred_element_type=F32)
    momentum_ref[...] = (blended_ref[...].astype(F32) - 0.1 * feedback).astype(BF16)


def feedback(blended, ortho, low):
    rows, cols = blended.shape
    rank = ortho.shape[1]
    steps = 4
    block = rows // steps
    tile = pl.BlockSpec((block, cols), lambda i: (i, 0))
    return pl.pallas_call(
        feedback_body,
        grid=(steps,),
        in_specs=[tile, pl.BlockSpec((block, rank), lambda i: (i, 0)), pl.BlockSpec((cols, rank), lambda i: (0, 0))],
        out_specs=tile,
        out_shape=shape((rows, cols), BF16),
        compiler_params=pltpu.CompilerParams(vmem_limit_bytes=24 << 20),
        name="feedback",
    )(blended, ortho, low)


def update_body(ortho_ref, right_ref, colsq_ref, update_ref, basis_ref):
    @pl.when(pl.program_id(0) == 0)
    def _():
        colsq = colsq_ref[0, 0:1, :]
        for i in range(1, colsq_ref.shape[0]):
            colsq = colsq + colsq_ref[i, 0:1, :]
        basis_ref[...] = (right_ref[...] * lax.rsqrt(colsq + 1e-06)).astype(BF16)

    product = lax.dot_general(ortho_ref[...], basis_ref[...], COLS_BY_COLS, preferred_element_type=F32)
    update_ref[...] = (SCALE * product).astype(BF16)


def update(ortho, right, colsq):
    rows, rank = ortho.shape
    cols = right.shape[0]
    steps = 4
    block = rows // steps
    return pl.pallas_call(
        update_body,
        grid=(steps,),
        in_specs=[
            pl.BlockSpec((block, rank), lambda i: (i, 0)),
            pl.BlockSpec((cols, rank), lambda i: (0, 0)),
            pl.BlockSpec(colsq.shape, lambda i: (0, 0, 0)),
        ],
        out_specs=[pl.BlockSpec((block, cols), lambda i: (i, 0)), pl.BlockSpec((cols, rank), lambda i: (0, 0))],
        out_shape=[shape((rows, cols), BF16), shape((cols, rank), BF16)],
        compiler_params=pltpu.CompilerParams(vmem_limit_bytes=24 << 20),
        name="update",
    )(ortho, right, colsq)


def on_device(momentum, gradient, basis, n_fsdp, n_tp):
    rank = basis.shape[1]
    rows, cols = momentum.shape
    some, block = rank // n_fsdp, cols // n_fsdp

    def exchange(parts, axis):
        return lax.all_to_all(parts, axis, 0, 0, tiled=True)

    blended, left = blend(momentum, gradient, basis)
    parts = exchange(left.reshape(n_tp, rows // n_tp, rank), "tp")
    spread = call(left_sum_body, shape(parts.shape, BF16), "left_sum", parts)
    left = exchange(spread, "tp").reshape(rows, rank)

    sent = shape((n_fsdp, 3 * some + block, rank), BF16)
    parts = call(project_body, sent, "project", blended, left, scratch=[pltpu.VMEM((cols, rank), F32)])
    gram, proj = call(
        project_sum_body,
        [shape((n_fsdp, some, rank)), shape((n_fsdp, block, rank), BF16)],
        "project_sum",
        exchange(parts, "fsdp"),
    )
    gram, proj = lax.optimization_barrier((exchange(gram, "fsdp"), proj))
    inverse, ortho = call(
        inverse_factor_body,
        [shape((rank, rank)), shape((rows, rank), BF16)],
        "inverse_factor",
        gram.reshape(rank, rank),
        left,
        flops=10**10,
    )
    right, low, colsq = call(
        right_body,
        [shape((cols, rank)), shape((cols, rank), BF16), shape((n_tp, 8, rank))],
        "right",
        exchange(proj, "fsdp").reshape(cols, rank),
        inverse,
    )
    colsq = exchange(colsq, "tp")
    momentum_next = feedback(blended, ortho, low)
    update_next, basis_next = update(ortho, right, colsq)
    return momentum_next, basis_next, update_next


def solution(mesh):
    body = functools.partial(on_device, n_fsdp=mesh.shape["fsdp"], n_tp=mesh.shape["tp"])
    return jax.shard_map(
        body,
        mesh=mesh,
        in_specs=(P("fsdp", "tp"), P("fsdp", "tp"), P("tp", None)),
        out_specs=(P("fsdp", "tp"), P("tp", None), P("fsdp", "tp")),
        check_vma=False,
    )
```

```python
import functools

import jax
import jax.numpy as jnp
from jax import lax
from jax.experimental import pallas as pl
from jax.experimental.pallas import tpu as pltpu
from jax.sharding import PartitionSpec as P

M_ROWS = 8192
N_COLS = 26624
RANK = 256
SCALE = (M_ROWS * N_COLS / RANK) ** 0.5
F32, BF16 = jnp.float32, jnp.bfloat16
PANEL = 64
VMEM = pl.BlockSpec(memory_space=pltpu.VMEM)
HBM = pl.BlockSpec(memory_space=pltpu.HBM)
TERMS = 2
ROWS_BY_ROWS = (((0,), (0,)), ((), ()))
COLS_BY_COLS = (((1,), (1,)), ((), ()))


def iota(shape, dim):
    return lax.broadcasted_iota(jnp.int32, shape, dim)


def shape(dims, dtype=F32):
    return jax.ShapeDtypeStruct(dims, dtype)


def held(dims, dtype=F32):
    return pltpu.VMEM(dims, dtype)


def call(body, out, name, *args, scratch=(), flops=0, out_specs=None):
    many = isinstance(out, (list, tuple))
    return pl.pallas_call(
        body,
        out_shape=out,
        in_specs=[VMEM] * len(args),
        out_specs=out_specs or ([VMEM] * len(out) if many else VMEM),
        scratch_shapes=list(scratch),
        compiler_params=pltpu.CompilerParams(vmem_limit_bytes=24 << 20),
        cost_estimate=pl.CostEstimate(flops=flops, bytes_accessed=1 << 20, transcendentals=0),
        name=name,
    )(*(pltpu.with_memory_space_constraint(a, pltpu.VMEM) for a in args))


def split(value):
    high = value.astype(BF16)
    rest = value - high.astype(F32)
    mid = rest.astype(BF16)
    return high, mid, (rest - mid.astype(F32)).astype(BF16)


def left_terms(value, axis):
    high, mid, low = split(value)
    return jnp.concatenate([high, high, mid, mid, high, low], axis=axis)


def right_terms(value):
    high, mid, low = split(value)
    return jnp.concatenate([high, mid, high, mid, low, high], axis=0)


def pieces_of(cols):
    cuts = [0, -(-cols // 384) * 128, -(-2 * cols // 384) * 128, cols]
    return list(zip(cuts[:-1], cuts[1:]))


def blend_body(momentum_ref, gradient_ref, basis_ref, blended_ref, left_ref, m_ref, g_ref, b_ref, sems):
    pieces = []
    for i, (lo, hi) in enumerate(pieces_of(blended_ref.shape[1])):
        lanes, rows = (slice(None), pl.ds(lo, hi - lo)), (pl.ds(lo, hi - lo), slice(None))
        copies = [
            pltpu.make_async_copy(src.at[at], dst.at[at], sems.at[3 * i + k])
            for k, (src, dst, at) in enumerate(
                ((momentum_ref, m_ref, lanes), (gradient_ref, g_ref, lanes), (basis_ref, b_ref, rows))
            )
        ]
        for copy in copies:
            copy.start()
        pieces.append((lo, hi, copies))
    left = None
    for lo, hi, copies in pieces:
        for copy in copies:
            copy.wait()
        blended = (m_ref[:, lo:hi].astype(F32) + g_ref[:, lo:hi].astype(F32)).astype(BF16)
        blended_ref[:, lo:hi] = blended
        part = jnp.dot(blended, b_ref[lo:hi, :], preferred_element_type=F32)
        left = part if left is None else left + part
    left_ref[...] = left.astype(BF16)


def blend(momentum, gradient, basis):
    rows, cols = momentum.shape
    rank = basis.shape[1]
    return pl.pallas_call(
        blend_body,
        out_shape=[held((rows, cols), BF16), held((rows, rank), BF16)],
        in_specs=[HBM] * 3,
        out_specs=[VMEM] * 2,
        scratch_shapes=[
            pltpu.VMEM((rows, cols), BF16),
            pltpu.VMEM((rows, cols), BF16),
            pltpu.VMEM((cols, rank), BF16),
            pltpu.SemaphoreType.DMA((9,)),
        ],
        compiler_params=pltpu.CompilerParams(vmem_limit_bytes=24 << 20),
        name="blend",
    )(*(pltpu.with_memory_space_constraint(a, pltpu.HBM) for a in (momentum, gradient, basis)))


def left_sum_body(parts_ref, out_ref):
    total = parts_ref[0].astype(F32)
    for i in range(1, parts_ref.shape[0]):
        total = total + parts_ref[i].astype(F32)
    low = total.astype(BF16)
    for i in range(out_ref.shape[0]):
        out_ref[i] = low


def project_body(blended_ref, left_ref, out_ref, work_ref):
    parts = out_ref.shape[0]
    rank = left_ref.shape[1]
    some = rank // parts
    block = blended_ref.shape[1] // parts
    left = left_ref[...]
    gram = split(lax.dot_general(left, left, ROWS_BY_ROWS, preferred_element_type=F32))[:TERMS]
    work_ref[...] = lax.dot_general(blended_ref[...], left, ROWS_BY_ROWS, preferred_element_type=F32)
    for f in range(parts):
        for i, term in enumerate(gram):
            out_ref[f, i * some : (i + 1) * some, :] = term[f * some : (f + 1) * some]
        out_ref[f, TERMS * some :, :] = work_ref[f * block : (f + 1) * block, :].astype(BF16)


def project_sum_body(parts_ref, gram_ref, proj_ref):
    some = gram_ref.shape[1]
    total = parts_ref[0].astype(F32)
    for i in range(1, parts_ref.shape[0]):
        total = total + parts_ref[i].astype(F32)
    gram = total[some : 2 * some] + total[:some]
    low = total[TERMS * some :].astype(BF16)
    for i in range(gram_ref.shape[0]):
        gram_ref[i] = gram
        proj_ref[i] = low


def diag_inverse(block):
    b = block.shape[0]
    n, width = b // 8, 2 * b
    eye = iota((b, b), 0) == iota((b, b), 1)
    aug = jnp.concatenate([block, jnp.where(eye, 1.0, 0.0)], axis=1)
    sub = iota((8, width), 0)
    rows = [aug[8 * i : 8 * i + 8] for i in range(n)]

    def spread(value, m):
        return jnp.broadcast_to(value[m : m + 1], (8, width))

    for g in range(n):
        cols = [
            [jnp.broadcast_to(rows[v][:, 8 * g + k : 8 * g + k + 1], (8, width)) for v in range(g, n)] for k in range(8)
        ]
        own, pivots, updates = rows[g], jnp.zeros((8, width), F32), []
        for m in range(0, 8, 2):
            first, second = cols[m], cols[m + 1]
            a, c, d = spread(first[0], m), spread(first[0], m + 1), spread(second[0], m + 1)
            det = a * d - c * c
            one_a, one_det = 1.0 / a, 1.0 / det
            pivots = jnp.where(sub == m, a, jnp.where(sub == m + 1, det * one_a, pivots))
            ia, ic, id_ = d * one_det, c * one_det, a * one_det
            below = sub > m + 1
            f0, f1 = jnp.where(below, first[0], 0.0), jnp.where(below, second[0], 0.0)

            def solved(value):
                x0, x1 = spread(value, m), spread(value, m + 1)
                return ia * x0 - ic * x1, id_ * x1 - ic * x0

            s0, s1 = solved(own)
            own = own - (f0 * s0 + f1 * s1) - jnp.where(sub == m + 1, c * one_a * spread(own, m), 0.0)
            updates += [(first[1:], s0), (second[1:], s1)]
            for k in range(m + 2, 8):
                t0, t1 = solved(cols[k][0])
                cols[k][0] = cols[k][0] - (f0 * t0 + f1 * t1)
                for v in range(1, n - g):
                    cols[k][v] = cols[k][v] - (first[v] * t0 + second[v] * t1)
        rows[g] = own * lax.rsqrt(pivots)
        for v in range(1, n - g):
            rows[g + v] = rows[g + v] - sum(col[v - 1] * s for col, s in updates)
    return jnp.concatenate(rows, axis=0)[:, b:]


def inverse_factor(gram, inv_ref):
    rank = gram.shape[0]
    row, col = iota((rank, rank), 0), iota((rank, rank), 1)
    inv_ref[...] = gram + jnp.where(row == col, 0.001, 0.0)
    lanes = iota((1, rank), 1)
    for p in range(0, rank, PANEL):
        q = p + PANEL
        inverse = diag_inverse(inv_ref[p:q, p:q])
        full = jnp.dot(left_terms(inverse, 1), right_terms(inv_ref[p:q, :]), preferred_element_type=F32)
        pieces = [full[:, :p]] if p else []
        pieces.append(inverse)
        if q < rank:
            pieces.append(full[:, q:])
        panel = jnp.concatenate(pieces, axis=1)
        inv_ref[p:q, :] = panel
        if q < rank:
            change = lax.dot_general(
                left_terms(panel[:, q:], 0), right_terms(panel), ROWS_BY_ROWS, preferred_element_type=F32
            )
            inv_ref[q:, :] = jnp.where((lanes >= p) & (lanes < q), 0.0, inv_ref[q:, :]) - change
    inv_ref[...] = jnp.where(row >= col, inv_ref[...], 0.0)


def by_inverse(low, inverse):
    n = inverse.shape[0]
    terms = jnp.concatenate(split(inverse)[:TERMS], axis=0)
    parts = lax.dot_general(low, terms, COLS_BY_COLS, preferred_element_type=F32)
    return parts[:, :n] + parts[:, n:]


def inverse_factor_body(gram_ref, inv_ref):
    inverse_factor(gram_ref[...], inv_ref)


def colsq_body(proj_ref, inv_ref, colsq_ref):
    right = by_inverse(proj_ref[...], inv_ref[...])
    colsq_ref[...] = jnp.broadcast_to(jnp.sum(right * right, axis=0)[None, None, :], colsq_ref.shape)


def feedback_body(blended_ref, left_ref, proj_ref, inv_ref, momentum_ref, ortho_ref):
    ortho_ref[...] = by_inverse(left_ref[...], inv_ref[...]).astype(BF16)
    right = by_inverse(proj_ref[...], inv_ref[...])
    feedback = lax.dot_general(ortho_ref[...], right.astype(BF16), COLS_BY_COLS, preferred_element_type=F32)
    momentum_ref[...] = (blended_ref[...].astype(F32) - 0.1 * feedback).astype(BF16)


def update_body(ortho_ref, proj_ref, inv_ref, colsq_ref, update_ref, basis_ref, product_ref, next_ref, sems):
    colsq = colsq_ref[0, 0:1, :]
    for i in range(1, colsq_ref.shape[0]):
        colsq = colsq + colsq_ref[i, 0:1, :]
    scale = lax.rsqrt(colsq + 1e-06)
    inverse, ortho, copies = inv_ref[...], ortho_ref[...], []
    for lo, hi in pieces_of(product_ref.shape[1]):
        rows, lanes = (pl.ds(lo, hi - lo), slice(None)), (slice(None), pl.ds(lo, hi - lo))
        basis = (by_inverse(proj_ref[lo:hi, :], inverse) * scale).astype(BF16)
        next_ref[lo:hi, :] = basis
        copies.append(pltpu.make_async_copy(next_ref.at[rows], basis_ref.at[rows], sems.at[len(copies)]))
        copies[-1].start()
        product = lax.dot_general(ortho, basis, COLS_BY_COLS, preferred_element_type=F32)
        product_ref[:, lo:hi] = (SCALE * product).astype(BF16)
        copies.append(pltpu.make_async_copy(product_ref.at[lanes], update_ref.at[lanes], sems.at[len(copies)]))
        copies[-1].start()
    for copy in copies:
        copy.wait()


def on_device(momentum, gradient, basis, n_fsdp, n_tp):
    rank = basis.shape[1]
    rows, cols = momentum.shape
    some, block = rank // n_fsdp, cols // n_fsdp

    def exchange(parts, axis):
        return lax.all_to_all(parts, axis, 0, 0, tiled=True)

    blended, left = blend(momentum, gradient, basis)
    parts = exchange(left.reshape(n_tp, rows // n_tp, rank), "tp")
    spread = call(left_sum_body, held(parts.shape, BF16), "left_sum", parts)
    left = exchange(spread, "tp").reshape(rows, rank)

    sent = held((n_fsdp, TERMS * some + block, rank), BF16)
    parts = call(project_body, sent, "project", blended, left, scratch=[pltpu.VMEM((cols, rank), F32)])
    gram, proj = call(
        project_sum_body,
        [held((n_fsdp, some, rank)), pltpu.HBM((n_fsdp, block, rank), BF16)],
        "project_sum",
        exchange(parts, "fsdp"),
    )
    gram, proj = lax.optimization_barrier((exchange(gram, "fsdp"), proj))
    inverse = call(inverse_factor_body, held((rank, rank)), "inverse_factor", gram.reshape(rank, rank), flops=10**10)
    proj = exchange(proj, "fsdp").reshape(cols, rank)
    colsq = exchange(call(colsq_body, held((n_tp, 8, rank)), "colsq", proj, inverse), "tp")
    momentum_next, ortho = call(
        feedback_body,
        [shape((rows, cols), BF16), held((rows, rank), BF16)],
        "feedback",
        blended,
        left,
        proj,
        inverse,
    )
    update_next, basis_next = call(
        update_body,
        [pltpu.HBM((rows, cols), BF16), pltpu.HBM((cols, rank), BF16)],
        "update",
        ortho,
        proj,
        inverse,
        colsq,
        scratch=[pltpu.VMEM((rows, cols), BF16), pltpu.VMEM((cols, rank), BF16), pltpu.SemaphoreType.DMA((6,))],
        out_specs=[HBM, HBM],
    )
    return momentum_next, basis_next, update_next


def solution(mesh):
    body = functools.partial(on_device, n_fsdp=mesh.shape["fsdp"], n_tp=mesh.shape["tp"])
    return jax.shard_map(
        body,
        mesh=mesh,
        in_specs=(P("fsdp", "tp"), P("fsdp", "tp"), P("tp", None)),
        out_specs=(P("fsdp", "tp"), P("tp", None), P("fsdp", "tp")),
        check_vma=False,
    )
```

```python
import functools

import jax
import jax.numpy as jnp
from jax import lax
from jax.experimental import pallas as pl
from jax.experimental.pallas import tpu as pltpu
from jax.sharding import PartitionSpec as P

M_ROWS = 8192
N_COLS = 26624
RANK = 256
SCALE = (M_ROWS * N_COLS / RANK) ** 0.5
F32, BF16 = jnp.float32, jnp.bfloat16
PANEL = 64
VMEM = pl.BlockSpec(memory_space=pltpu.VMEM)
HBM = pl.BlockSpec(memory_space=pltpu.HBM)
TERMS = 2
ROWS_BY_ROWS = (((0,), (0,)), ((), ()))
COLS_BY_COLS = (((1,), (1,)), ((), ()))
ROWS_BY_COLS = (((1,), (0,)), ((), ()))


def iota(shape, dim):
    return lax.broadcasted_iota(jnp.int32, shape, dim)


def shape(dims, dtype=F32):
    return jax.ShapeDtypeStruct(dims, dtype)


def held(dims, dtype=F32):
    return pltpu.VMEM(dims, dtype)


def call(body, out, name, *args, scratch=(), flops=0, out_specs=None):
    many = isinstance(out, (list, tuple))
    return pl.pallas_call(
        body,
        out_shape=out,
        in_specs=[VMEM] * len(args),
        out_specs=out_specs or ([VMEM] * len(out) if many else VMEM),
        scratch_shapes=list(scratch),
        compiler_params=pltpu.CompilerParams(vmem_limit_bytes=24 << 20),
        cost_estimate=pl.CostEstimate(flops=flops, bytes_accessed=1 << 20, transcendentals=0),
        name=name,
    )(*(pltpu.with_memory_space_constraint(a, pltpu.VMEM) for a in args))


def split(value):
    high = value.astype(BF16)
    rest = value - high.astype(F32)
    mid = rest.astype(BF16)
    return high, mid, (rest - mid.astype(F32)).astype(BF16)


def left_terms(value, axis):
    high, mid, low = split(value)
    return jnp.concatenate([high, high, mid, mid, high, low], axis=axis)


def right_terms(value):
    high, mid, low = split(value)
    return jnp.concatenate([high, mid, high, mid, low, high], axis=0)


def pieces_of(cols):
    cuts = [0, -(-cols // 384) * 128, -(-2 * cols // 384) * 128, cols]
    return list(zip(cuts[:-1], cuts[1:]))


def blend_body(momentum_ref, gradient_ref, basis_ref, blended_ref, left_ref, m_ref, g_ref, b_ref, sems):
    pieces = []
    for i, (lo, hi) in enumerate(pieces_of(blended_ref.shape[1])):
        lanes, rows = (slice(None), pl.ds(lo, hi - lo)), (pl.ds(lo, hi - lo), slice(None))
        copies = [
            pltpu.make_async_copy(src.at[at], dst.at[at], sems.at[3 * i + k])
            for k, (src, dst, at) in enumerate(
                ((momentum_ref, m_ref, lanes), (gradient_ref, g_ref, lanes), (basis_ref, b_ref, rows))
            )
        ]
        for copy in copies:
            copy.start()
        pieces.append((lo, hi, copies))
    left = None
    for lo, hi, copies in pieces:
        for copy in copies:
            copy.wait()
        blended = (m_ref[:, lo:hi].astype(F32) + g_ref[:, lo:hi].astype(F32)).astype(BF16)
        blended_ref[:, lo:hi] = blended
        part = jnp.dot(blended, b_ref[lo:hi, :], preferred_element_type=F32)
        left = part if left is None else left + part
    left_ref[...] = left.astype(BF16)


def blend(momentum, gradient, basis):
    rows, cols = momentum.shape
    rank = basis.shape[1]
    return pl.pallas_call(
        blend_body,
        out_shape=[held((rows, cols), BF16), held((rows, rank), BF16)],
        in_specs=[HBM] * 3,
        out_specs=[VMEM] * 2,
        scratch_shapes=[
            pltpu.VMEM((rows, cols), BF16),
            pltpu.VMEM((rows, cols), BF16),
            pltpu.VMEM((cols, rank), BF16),
            pltpu.SemaphoreType.DMA((9,)),
        ],
        compiler_params=pltpu.CompilerParams(vmem_limit_bytes=24 << 20),
        name="blend",
    )(*(pltpu.with_memory_space_constraint(a, pltpu.HBM) for a in (momentum, gradient, basis)))


def left_sum_body(parts_ref, out_ref):
    total = parts_ref[0].astype(F32)
    for i in range(1, parts_ref.shape[0]):
        total = total + parts_ref[i].astype(F32)
    low = total.astype(BF16)
    for i in range(out_ref.shape[0]):
        out_ref[i] = low


def project_body(blended_ref, left_ref, out_ref, work_ref):
    parts = out_ref.shape[0]
    rank = left_ref.shape[1]
    some = rank // parts
    block = blended_ref.shape[1] // parts
    left = left_ref[...]
    gram = split(lax.dot_general(left, left, ROWS_BY_ROWS, preferred_element_type=F32))[:TERMS]
    work_ref[...] = lax.dot_general(blended_ref[...], left, ROWS_BY_ROWS, preferred_element_type=F32)
    for f in range(parts):
        for i, term in enumerate(gram):
            out_ref[f, i * some : (i + 1) * some, :] = term[f * some : (f + 1) * some]
        out_ref[f, TERMS * some :, :] = work_ref[f * block : (f + 1) * block, :].astype(BF16)


def project_sum_body(parts_ref, out_ref, *, some):
    total = parts_ref[0].astype(F32)
    for i in range(1, parts_ref.shape[0]):
        total = total + parts_ref[i].astype(F32)
    high, low, _ = split(total[some : 2 * some] + total[:some])
    merged = jnp.concatenate([high, low, total[TERMS * some :].astype(BF16)], axis=0)
    for i in range(out_ref.shape[0]):
        out_ref[i] = merged


def diag_inverse(block):
    b = block.shape[0]
    n, width = b // 8, 2 * b
    eye = iota((b, b), 0) == iota((b, b), 1)
    aug = jnp.concatenate([block, jnp.where(eye, 1.0, 0.0)], axis=1)
    sub = iota((8, width), 0)
    rows = [aug[8 * i : 8 * i + 8] for i in range(n)]

    def spread(value, m):
        return jnp.broadcast_to(value[m : m + 1], (8, width))

    for g in range(n):
        cols = [
            [jnp.broadcast_to(rows[v][:, 8 * g + k : 8 * g + k + 1], (8, width)) for v in range(g, n)] for k in range(8)
        ]
        own, pivots, updates = rows[g], jnp.zeros((8, width), F32), []
        for m in range(0, 8, 2):
            first, second = cols[m], cols[m + 1]
            a, c, d = spread(first[0], m), spread(first[0], m + 1), spread(second[0], m + 1)
            det = a * d - c * c
            one_a, one_det = 1.0 / a, 1.0 / det
            pivots = jnp.where(sub == m, a, jnp.where(sub == m + 1, det * one_a, pivots))
            ia, ic, id_ = d * one_det, c * one_det, a * one_det
            below = sub > m + 1
            f0, f1 = jnp.where(below, first[0], 0.0), jnp.where(below, second[0], 0.0)

            def solved(value):
                x0, x1 = spread(value, m), spread(value, m + 1)
                return ia * x0 - ic * x1, id_ * x1 - ic * x0

            s0, s1 = solved(own)
            own = own - (f0 * s0 + f1 * s1) - jnp.where(sub == m + 1, c * one_a * spread(own, m), 0.0)
            updates += [(first[1:], s0), (second[1:], s1)]
            for k in range(m + 2, 8):
                t0, t1 = solved(cols[k][0])
                cols[k][0] = cols[k][0] - (f0 * t0 + f1 * t1)
                for v in range(1, n - g):
                    cols[k][v] = cols[k][v] - (first[v] * t0 + second[v] * t1)
        rows[g] = own * lax.rsqrt(pivots)
        for v in range(1, n - g):
            rows[g + v] = rows[g + v] - sum(col[v - 1] * s for col, s in updates)
    return jnp.concatenate(rows, axis=0)[:, b:]


def inverse_factor(gram, inv_ref):
    rank = gram.shape[0]
    row, col = iota((rank, rank), 0), iota((rank, rank), 1)
    inv_ref[...] = gram + jnp.where(row == col, 0.001, 0.0)
    lanes = iota((1, rank), 1)
    for p in range(0, rank, PANEL):
        q = p + PANEL
        inverse = diag_inverse(inv_ref[p:q, p:q])
        full = jnp.dot(left_terms(inverse, 1), right_terms(inv_ref[p:q, :]), preferred_element_type=F32)
        pieces = [full[:, :p]] if p else []
        pieces.append(inverse)
        if q < rank:
            pieces.append(full[:, q:])
        panel = jnp.concatenate(pieces, axis=1)
        inv_ref[p:q, :] = panel
        if q < rank:
            change = lax.dot_general(
                left_terms(panel[:, q:], 0), right_terms(panel), ROWS_BY_ROWS, preferred_element_type=F32
            )
            inv_ref[q:, :] = jnp.where((lanes >= p) & (lanes < q), 0.0, inv_ref[q:, :]) - change
    inv_ref[...] = jnp.where(row >= col, inv_ref[...], 0.0)


def by_inverse(low, inverse):
    n = inverse.shape[0]
    terms = jnp.concatenate(split(inverse)[:TERMS], axis=0)
    parts = lax.dot_general(low, terms, COLS_BY_COLS, preferred_element_type=F32)
    return parts[:, :n] + parts[:, n:]


def product(a, b, dims, terms):
    if terms == 1:
        return lax.dot_general(a.astype(BF16), b.astype(BF16), dims, preferred_element_type=F32)
    (a_high, a_low, _), (b_high, b_low, _) = split(a), split(b)
    a = jnp.concatenate([a_high, a_high, a_low], axis=dims[0][0][0])
    b = jnp.concatenate([b_high, b_low, b_high], axis=dims[0][1][0])
    return lax.dot_general(a, b, dims, preferred_element_type=F32)


def refined_factor(gram, inv_ref):
    rank = gram.shape[0]
    row, col = iota((rank, rank), 0), iota((rank, rank), 1)
    eye = row == col
    gram = gram + jnp.where(eye, 0.001, 0.0)
    diag = jnp.where(eye, gram, 0.0)
    scale = lax.rsqrt(jnp.sum(diag, axis=0, keepdims=True))
    gram = gram * lax.rsqrt(jnp.sum(diag, axis=1, keepdims=True)) * scale
    inverse = jnp.where(eye, 1.0, jnp.where(row > col, -gram, 0.0))
    for terms in (1, 2, 2):
        error = product(product(inverse, gram, ROWS_BY_COLS, terms), inverse, COLS_BY_COLS, terms)
        error = error - jnp.where(eye, 1.0, 0.0)
        lower = jnp.where(row > col, error, jnp.where(eye, 0.5 * error, 0.0))
        inverse = inverse - product(lower, inverse, ROWS_BY_COLS, terms)
    inv_ref[...] = inverse * scale
    return jnp.sum(error * error)


def factor_body(parts_ref, inv_ref, proj_ref, colsq_ref):
    rank = inv_ref.shape[0]
    some = rank // parts_ref.shape[0]
    gram = parts_ref[:, :some, :].astype(F32) + parts_ref[:, some : 2 * some, :].astype(F32)
    gram = gram.reshape(rank, rank)
    proj_ref[...] = parts_ref[:, TERMS * some :, :].astype(F32).reshape(proj_ref.shape).astype(BF16)

    taken = refined_factor(gram, inv_ref)

    @pl.when(jnp.logical_not(taken < 1e-4))
    def _():
        inverse_factor(gram, inv_ref)

    right = by_inverse(proj_ref[...], inv_ref[...])
    colsq = jnp.broadcast_to(jnp.sum(right * right, axis=0, keepdims=True), colsq_ref.shape[1:])
    for i in range(colsq_ref.shape[0]):
        colsq_ref[i] = colsq


def feedback_body(blended_ref, left_ref, proj_ref, inv_ref, momentum_ref, ortho_ref):
    ortho_ref[...] = by_inverse(left_ref[...], inv_ref[...]).astype(BF16)
    right = by_inverse(proj_ref[...], inv_ref[...])
    feedback = lax.dot_general(ortho_ref[...], right.astype(BF16), COLS_BY_COLS, preferred_element_type=F32)
    momentum_ref[...] = (blended_ref[...].astype(F32) - 0.1 * feedback).astype(BF16)


def update_body(ortho_ref, proj_ref, inv_ref, colsq_ref, update_ref, basis_ref, product_ref, next_ref, sems):
    colsq = colsq_ref[0, 0:1, :]
    for i in range(1, colsq_ref.shape[0]):
        colsq = colsq + colsq_ref[i, 0:1, :]
    scale = lax.rsqrt(colsq + 1e-06)
    inverse, ortho, copies = inv_ref[...], ortho_ref[...], []
    for lo, hi in pieces_of(product_ref.shape[1]):
        rows, lanes = (pl.ds(lo, hi - lo), slice(None)), (slice(None), pl.ds(lo, hi - lo))
        basis = (by_inverse(proj_ref[lo:hi, :], inverse) * scale).astype(BF16)
        next_ref[lo:hi, :] = basis
        copies.append(pltpu.make_async_copy(next_ref.at[rows], basis_ref.at[rows], sems.at[len(copies)]))
        copies[-1].start()
        product = lax.dot_general(ortho, basis, COLS_BY_COLS, preferred_element_type=F32)
        product_ref[:, lo:hi] = (SCALE * product).astype(BF16)
        copies.append(pltpu.make_async_copy(product_ref.at[lanes], update_ref.at[lanes], sems.at[len(copies)]))
        copies[-1].start()
    for copy in copies:
        copy.wait()


def on_device(momentum, gradient, basis, n_fsdp, n_tp):
    rank = basis.shape[1]
    rows, cols = momentum.shape
    some, block = rank // n_fsdp, cols // n_fsdp

    def exchange(parts, axis):
        return lax.all_to_all(parts, axis, 0, 0, tiled=True)

    blended, left = blend(momentum, gradient, basis)
    parts = exchange(left.reshape(n_tp, rows // n_tp, rank), "tp")
    spread = call(left_sum_body, held(parts.shape, BF16), "left_sum", parts)
    left = exchange(spread, "tp").reshape(rows, rank)

    sent = held((n_fsdp, TERMS * some + block, rank), BF16)
    parts = call(project_body, sent, "project", blended, left, scratch=[pltpu.VMEM((cols, rank), F32)])
    merged = call(
        functools.partial(project_sum_body, some=some), held(parts.shape, BF16), "project_sum", exchange(parts, "fsdp")
    )
    inverse, proj, colsq = call(
        factor_body,
        [held((rank, rank)), held((cols, rank), BF16), held((n_tp, 8, rank))],
        "factor",
        exchange(merged, "fsdp"),
    )
    colsq = exchange(colsq, "tp")
    momentum_next, ortho = call(
        feedback_body,
        [shape((rows, cols), BF16), held((rows, rank), BF16)],
        "feedback",
        blended,
        left,
        proj,
        inverse,
    )
    update_next, basis_next = call(
        update_body,
        [pltpu.HBM((rows, cols), BF16), pltpu.HBM((cols, rank), BF16)],
        "update",
        ortho,
        proj,
        inverse,
        colsq,
        scratch=[pltpu.VMEM((rows, cols), BF16), pltpu.VMEM((cols, rank), BF16), pltpu.SemaphoreType.DMA((6,))],
        out_specs=[HBM, HBM],
    )
    return momentum_next, basis_next, update_next


def solution(mesh):
    body = functools.partial(on_device, n_fsdp=mesh.shape["fsdp"], n_tp=mesh.shape["tp"])
    return jax.shard_map(
        body,
        mesh=mesh,
        in_specs=(P("fsdp", "tp"), P("fsdp", "tp"), P("tp", None)),
        out_specs=(P("fsdp", "tp"), P("tp", None), P("fsdp", "tp")),
        check_vma=False,
    )
```

```python
import functools

import jax
import jax.numpy as jnp
from jax import lax
from jax.experimental import pallas as pl
from jax.experimental.pallas import tpu as pltpu
from jax.sharding import PartitionSpec as P

M_ROWS = 8192
N_COLS = 26624
RANK = 256
SCALE = (M_ROWS * N_COLS / RANK) ** 0.5
F32, BF16 = jnp.float32, jnp.bfloat16
PANEL = 64
VMEM = pl.BlockSpec(memory_space=pltpu.VMEM)
HBM = pl.BlockSpec(memory_space=pltpu.HBM)
TERMS = 2
ORDERS = {
    "fsdp": [2, 11, 3, 10, 0, 4, 15, 7, 12, 1, 13, 5, 14, 9, 6, 8],
    "tp": [11, 15, 9, 1, 12, 2, 14, 10, 0, 4, 7, 6, 13, 5, 3, 8],
}
ROWS_BY_ROWS = (((0,), (0,)), ((), ()))
COLS_BY_COLS = (((1,), (1,)), ((), ()))
ROWS_BY_COLS = (((1,), (0,)), ((), ()))


def iota(shape, dim):
    return lax.broadcasted_iota(jnp.int32, shape, dim)


def shape(dims, dtype=F32):
    return jax.ShapeDtypeStruct(dims, dtype)


def held(dims, dtype=F32):
    return pltpu.VMEM(dims, dtype)


def call(body, out, name, *args, scratch=(), flops=0, out_specs=None):
    many = isinstance(out, (list, tuple))
    return pl.pallas_call(
        body,
        out_shape=out,
        in_specs=[VMEM] * len(args),
        out_specs=out_specs or ([VMEM] * len(out) if many else VMEM),
        scratch_shapes=list(scratch),
        compiler_params=pltpu.CompilerParams(vmem_limit_bytes=24 << 20),
        cost_estimate=pl.CostEstimate(flops=flops, bytes_accessed=1 << 20, transcendentals=0),
        name=name,
    )(*(pltpu.with_memory_space_constraint(a, pltpu.VMEM) for a in args))


def split(value):
    high = value.astype(BF16)
    rest = value - high.astype(F32)
    mid = rest.astype(BF16)
    return high, mid, (rest - mid.astype(F32)).astype(BF16)


def left_terms(value, axis):
    high, mid, low = split(value)
    return jnp.concatenate([high, high, mid, mid, high, low], axis=axis)


def right_terms(value):
    high, mid, low = split(value)
    return jnp.concatenate([high, mid, high, mid, low, high], axis=0)


def pieces_of(cols, eighths=(0, 3, 6, 8)):
    cuts = [-(-cols * e // 1024) * 128 for e in eighths[:-1]] + [cols]
    return list(zip(cuts[:-1], cuts[1:]))


def blend_body(momentum_ref, gradient_ref, basis_ref, blended_ref, left_ref, m_ref, g_ref, b_ref, sems):
    pieces = []
    for i, (lo, hi) in enumerate(pieces_of(blended_ref.shape[1])):
        lanes, rows = (slice(None), pl.ds(lo, hi - lo)), (pl.ds(lo, hi - lo), slice(None))
        copies = [
            pltpu.make_async_copy(src.at[at], dst.at[at], sems.at[3 * i + k])
            for k, (src, dst, at) in enumerate(
                ((momentum_ref, m_ref, lanes), (gradient_ref, g_ref, lanes), (basis_ref, b_ref, rows))
            )
        ]
        for copy in copies:
            copy.start()
        pieces.append((lo, hi, copies))
    left = None
    for lo, hi, copies in pieces:
        for copy in copies:
            copy.wait()
        blended = (m_ref[:, lo:hi].astype(F32) + g_ref[:, lo:hi].astype(F32)).astype(BF16)
        blended_ref[:, lo:hi] = blended
        part = jnp.dot(blended, b_ref[lo:hi, :], preferred_element_type=F32)
        left = part if left is None else left + part
    left_ref[...] = left.astype(BF16)


def blend(momentum, gradient, basis):
    rows, cols = momentum.shape
    rank = basis.shape[1]
    return pl.pallas_call(
        blend_body,
        out_shape=[held((rows, cols), BF16), held((rows, rank), BF16)],
        in_specs=[HBM] * 3,
        out_specs=[VMEM] * 2,
        scratch_shapes=[
            pltpu.VMEM((rows, cols), BF16),
            pltpu.VMEM((rows, cols), BF16),
            pltpu.VMEM((cols, rank), BF16),
            pltpu.SemaphoreType.DMA((9,)),
        ],
        compiler_params=pltpu.CompilerParams(vmem_limit_bytes=24 << 20),
        name="blend",
    )(*(pltpu.with_memory_space_constraint(a, pltpu.HBM) for a in (momentum, gradient, basis)))


def left_sum_body(parts_ref, out_ref):
    total = parts_ref[0].astype(F32)
    for i in range(1, parts_ref.shape[0]):
        total = total + parts_ref[i].astype(F32)
    low = total.astype(BF16)
    for i in range(out_ref.shape[0]):
        out_ref[i] = low


def project_body(blended_ref, left_ref, out_ref, work_ref):
    parts = out_ref.shape[0]
    rank = left_ref.shape[1]
    some = rank // parts
    block = blended_ref.shape[1] // parts
    left = left_ref[...]
    gram = split(lax.dot_general(left, left, ROWS_BY_ROWS, preferred_element_type=F32))[:TERMS]
    work_ref[...] = lax.dot_general(blended_ref[...], left, ROWS_BY_ROWS, preferred_element_type=F32)
    for f in range(parts):
        for i, term in enumerate(gram):
            out_ref[f, i * some : (i + 1) * some, :] = term[f * some : (f + 1) * some]
        out_ref[f, TERMS * some :, :] = work_ref[f * block : (f + 1) * block, :].astype(BF16)


def project_sum_body(parts_ref, out_ref, *, some):
    total = parts_ref[0].astype(F32)
    for i in range(1, parts_ref.shape[0]):
        total = total + parts_ref[i].astype(F32)
    high, low, _ = split(total[some : 2 * some] + total[:some])
    merged = jnp.concatenate([high, low, total[TERMS * some :].astype(BF16)], axis=0)
    for i in range(out_ref.shape[0]):
        out_ref[i] = merged


def diag_inverse(block):
    b = block.shape[0]
    n, width = b // 8, 2 * b
    eye = iota((b, b), 0) == iota((b, b), 1)
    aug = jnp.concatenate([block, jnp.where(eye, 1.0, 0.0)], axis=1)
    sub = iota((8, width), 0)
    rows = [aug[8 * i : 8 * i + 8] for i in range(n)]

    def spread(value, m):
        return jnp.broadcast_to(value[m : m + 1], (8, width))

    for g in range(n):
        cols = [
            [jnp.broadcast_to(rows[v][:, 8 * g + k : 8 * g + k + 1], (8, width)) for v in range(g, n)] for k in range(8)
        ]
        own, pivots, updates = rows[g], jnp.zeros((8, width), F32), []
        for m in range(0, 8, 2):
            first, second = cols[m], cols[m + 1]
            a, c, d = spread(first[0], m), spread(first[0], m + 1), spread(second[0], m + 1)
            det = a * d - c * c
            one_a, one_det = 1.0 / a, 1.0 / det
            pivots = jnp.where(sub == m, a, jnp.where(sub == m + 1, det * one_a, pivots))
            ia, ic, id_ = d * one_det, c * one_det, a * one_det
            below = sub > m + 1
            f0, f1 = jnp.where(below, first[0], 0.0), jnp.where(below, second[0], 0.0)

            def solved(value):
                x0, x1 = spread(value, m), spread(value, m + 1)
                return ia * x0 - ic * x1, id_ * x1 - ic * x0

            s0, s1 = solved(own)
            own = own - (f0 * s0 + f1 * s1) - jnp.where(sub == m + 1, c * one_a * spread(own, m), 0.0)
            updates += [(first[1:], s0), (second[1:], s1)]
            for k in range(m + 2, 8):
                t0, t1 = solved(cols[k][0])
                cols[k][0] = cols[k][0] - (f0 * t0 + f1 * t1)
                for v in range(1, n - g):
                    cols[k][v] = cols[k][v] - (first[v] * t0 + second[v] * t1)
        rows[g] = own * lax.rsqrt(pivots)
        for v in range(1, n - g):
            rows[g + v] = rows[g + v] - sum(col[v - 1] * s for col, s in updates)
    return jnp.concatenate(rows, axis=0)[:, b:]


def inverse_factor(gram, inv_ref):
    rank = gram.shape[0]
    row, col = iota((rank, rank), 0), iota((rank, rank), 1)
    inv_ref[...] = gram + jnp.where(row == col, 0.001, 0.0)
    lanes = iota((1, rank), 1)
    for p in range(0, rank, PANEL):
        q = p + PANEL
        inverse = diag_inverse(inv_ref[p:q, p:q])
        full = jnp.dot(left_terms(inverse, 1), right_terms(inv_ref[p:q, :]), preferred_element_type=F32)
        pieces = [full[:, :p]] if p else []
        pieces.append(inverse)
        if q < rank:
            pieces.append(full[:, q:])
        panel = jnp.concatenate(pieces, axis=1)
        inv_ref[p:q, :] = panel
        if q < rank:
            change = lax.dot_general(
                left_terms(panel[:, q:], 0), right_terms(panel), ROWS_BY_ROWS, preferred_element_type=F32
            )
            inv_ref[q:, :] = jnp.where((lanes >= p) & (lanes < q), 0.0, inv_ref[q:, :]) - change
    inv_ref[...] = jnp.where(row >= col, inv_ref[...], 0.0)


def by_inverse(low, inverse):
    terms = split(inverse)[:TERMS]
    return lax.dot_general(
        jnp.concatenate([low] * TERMS, axis=1), jnp.concatenate(terms, axis=1), COLS_BY_COLS, preferred_element_type=F32
    )


def product(a, b, dims, terms):
    if terms == 1:
        return lax.dot_general(a.astype(BF16), b.astype(BF16), dims, preferred_element_type=F32)
    (a_high, a_low, _), (b_high, b_low, _) = split(a), split(b)
    a = jnp.concatenate([a_high, a_high, a_low], axis=dims[0][0][0])
    b = jnp.concatenate([b_high, b_low, b_high], axis=dims[0][1][0])
    return lax.dot_general(a, b, dims, preferred_element_type=F32)


def refined_factor(gram, inv_ref):
    rank = gram.shape[0]
    row, col = iota((rank, rank), 0), iota((rank, rank), 1)
    eye = row == col
    gram = gram + jnp.where(eye, 0.001, 0.0)
    diag = jnp.where(eye, gram, 0.0)
    scale = lax.rsqrt(jnp.sum(diag, axis=0, keepdims=True))
    gram = gram * lax.rsqrt(jnp.sum(diag, axis=1, keepdims=True)) * scale
    inverse = jnp.where(eye, 1.0, jnp.where(row > col, -gram, 0.0))
    for terms in (1, 2, 2):
        error = product(product(inverse, gram, ROWS_BY_COLS, terms), inverse, COLS_BY_COLS, terms)
        error = error - jnp.where(eye, 1.0, 0.0)
        lower = jnp.where(row > col, error, jnp.where(eye, 0.5 * error, 0.0))
        inverse = inverse - product(lower, inverse, ROWS_BY_COLS, terms)
    inv_ref[...] = inverse * scale
    return jnp.sum(error * error)


def factor_body(parts_ref, inv_ref, proj_ref, colsq_ref):
    rank = inv_ref.shape[0]
    some = rank // parts_ref.shape[0]
    gram = parts_ref[:, :some, :].astype(F32) + parts_ref[:, some : 2 * some, :].astype(F32)
    gram = gram.reshape(rank, rank)
    proj_ref[...] = parts_ref[:, TERMS * some :, :].astype(F32).reshape(proj_ref.shape).astype(BF16)

    def spread_colsq():
        right = by_inverse(proj_ref[...], inv_ref[...])
        colsq = jnp.broadcast_to(jnp.sum(right * right, axis=0, keepdims=True), colsq_ref.shape[1:])
        for i in range(colsq_ref.shape[0]):
            colsq_ref[i] = colsq

    taken = refined_factor(gram, inv_ref)
    spread_colsq()

    @pl.when(jnp.logical_not(taken < 1e-4))
    def _():
        inverse_factor(gram, inv_ref)
        spread_colsq()


def feedback_body(blended_ref, left_ref, proj_ref, inv_ref, momentum_ref, ortho_ref):
    ortho_ref[...] = by_inverse(left_ref[...], inv_ref[...]).astype(BF16)
    right = by_inverse(proj_ref[...], inv_ref[...])
    feedback = lax.dot_general(ortho_ref[...], right.astype(BF16), COLS_BY_COLS, preferred_element_type=F32)
    momentum_ref[...] = (blended_ref[...].astype(F32) - 0.1 * feedback).astype(BF16)


def update_body(ortho_ref, proj_ref, inv_ref, colsq_ref, update_ref, basis_ref, product_ref, next_ref, sems):
    colsq = colsq_ref[0, 0:1, :]
    for i in range(1, colsq_ref.shape[0]):
        colsq = colsq + colsq_ref[i, 0:1, :]
    scale = lax.rsqrt(colsq + 1e-06)
    inverse, ortho, copies = inv_ref[...], ortho_ref[...], []
    for lo, hi in pieces_of(product_ref.shape[1], (0, 1, 3, 5, 8)):
        rows, lanes = (pl.ds(lo, hi - lo), slice(None)), (slice(None), pl.ds(lo, hi - lo))
        basis = (by_inverse(proj_ref[lo:hi, :], inverse) * scale).astype(BF16)
        next_ref[lo:hi, :] = basis
        copies.append(pltpu.make_async_copy(next_ref.at[rows], basis_ref.at[rows], sems.at[len(copies)]))
        copies[-1].start()
        product = lax.dot_general(ortho, basis, COLS_BY_COLS, preferred_element_type=F32)
        product_ref[:, lo:hi] = (SCALE * product).astype(BF16)
        copies.append(pltpu.make_async_copy(product_ref.at[lanes], update_ref.at[lanes], sems.at[len(copies)]))
        copies[-1].start()
    for copy in copies:
        copy.wait()


def on_device(momentum, gradient, basis, n_fsdp, n_tp):
    rank = basis.shape[1]
    rows, cols = momentum.shape
    some, block = rank // n_fsdp, cols // n_fsdp

    def exchange(parts, axis):
        return lax.all_to_all(parts, axis, 0, 0, tiled=True, axis_index_groups=[ORDERS[axis]])

    blended, left = blend(momentum, gradient, basis)
    parts = exchange(left.reshape(n_tp, rows // n_tp, rank), "tp")
    spread = call(left_sum_body, held(parts.shape, BF16), "left_sum", parts)
    left = exchange(spread, "tp").reshape(rows, rank)

    sent = held((n_fsdp, TERMS * some + block, rank), BF16)
    parts = call(project_body, sent, "project", blended, left, scratch=[pltpu.VMEM((cols, rank), F32)])
    merged = call(
        functools.partial(project_sum_body, some=some), held(parts.shape, BF16), "project_sum", exchange(parts, "fsdp")
    )
    inverse, proj, colsq = call(
        factor_body,
        [held((rank, rank)), held((cols, rank), BF16), held((n_tp, 8, rank))],
        "factor",
        exchange(merged, "fsdp"),
    )
    colsq = exchange(colsq, "tp")
    momentum_next, ortho = call(
        feedback_body,
        [shape((rows, cols), BF16), held((rows, rank), BF16)],
        "feedback",
        blended,
        left,
        proj,
        inverse,
    )
    update_next, basis_next = call(
        update_body,
        [pltpu.HBM((rows, cols), BF16), pltpu.HBM((cols, rank), BF16)],
        "update",
        ortho,
        proj,
        inverse,
        colsq,
        scratch=[pltpu.VMEM((rows, cols), BF16), pltpu.VMEM((cols, rank), BF16), pltpu.SemaphoreType.DMA((8,))],
        out_specs=[HBM, HBM],
    )
    return momentum_next, basis_next, update_next


def solution(mesh):
    body = functools.partial(on_device, n_fsdp=mesh.shape["fsdp"], n_tp=mesh.shape["tp"])
    return jax.shard_map(
        body,
        mesh=mesh,
        in_specs=(P("fsdp", "tp"), P("fsdp", "tp"), P("tp", None)),
        out_specs=(P("fsdp", "tp"), P("tp", None), P("fsdp", "tp")),
        check_vma=False,
    )
```

```python
import functools

import jax
import jax.numpy as jnp
from jax import lax
from jax.experimental import pallas as pl
from jax.experimental.pallas import tpu as pltpu
from jax.sharding import PartitionSpec as P

M_ROWS = 8192
N_COLS = 26624
RANK = 256
SCALE = (M_ROWS * N_COLS / RANK) ** 0.5
F32, BF16 = jnp.float32, jnp.bfloat16
PANEL = 64
VMEM = pl.BlockSpec(memory_space=pltpu.VMEM)
HBM = pl.BlockSpec(memory_space=pltpu.HBM)
TERMS = 2
ORDERS = {
    "fsdp": [
        [2, 11, 3, 10, 0, 4, 15, 7, 12, 1, 13, 5, 14, 9, 6, 8],
        [2, 8, 13, 12, 1, 9, 6, 5, 11, 4, 15, 3, 10, 7, 0, 14],
    ],
    "tp": [11, 15, 9, 1, 12, 2, 14, 10, 0, 4, 7, 6, 13, 5, 3, 8],
}
ROWS_BY_ROWS = (((0,), (0,)), ((), ()))
COLS_BY_COLS = (((1,), (1,)), ((), ()))
ROWS_BY_COLS = (((1,), (0,)), ((), ()))


def iota(shape, dim):
    return lax.broadcasted_iota(jnp.int32, shape, dim)


def shape(dims, dtype=F32):
    return jax.ShapeDtypeStruct(dims, dtype)


def held(dims, dtype=F32):
    return pltpu.VMEM(dims, dtype)


def call(body, out, name, *args, scratch=(), flops=0, out_specs=None):
    many = isinstance(out, (list, tuple))
    return pl.pallas_call(
        body,
        out_shape=out,
        in_specs=[VMEM] * len(args),
        out_specs=out_specs or ([VMEM] * len(out) if many else VMEM),
        scratch_shapes=list(scratch),
        compiler_params=pltpu.CompilerParams(vmem_limit_bytes=24 << 20),
        cost_estimate=pl.CostEstimate(flops=flops, bytes_accessed=1 << 20, transcendentals=0),
        name=name,
    )(*(pltpu.with_memory_space_constraint(a, pltpu.VMEM) for a in args))


def split(value):
    high = value.astype(BF16)
    rest = value - high.astype(F32)
    mid = rest.astype(BF16)
    return high, mid, (rest - mid.astype(F32)).astype(BF16)


def left_terms(value, axis):
    high, mid, low = split(value)
    return jnp.concatenate([high, high, mid, mid, high, low], axis=axis)


def right_terms(value):
    high, mid, low = split(value)
    return jnp.concatenate([high, mid, high, mid, low, high], axis=0)


def pieces_of(cols, eighths=(0, 3, 6, 8)):
    cuts = [-(-cols * e // 1024) * 128 for e in eighths[:-1]] + [cols]
    return list(zip(cuts[:-1], cuts[1:]))


def blend_body(momentum_ref, gradient_ref, basis_ref, blended_ref, left_ref, m_ref, g_ref, b_ref, sems):
    pieces = []
    for i, (lo, hi) in enumerate(pieces_of(blended_ref.shape[1])):
        lanes, rows = (slice(None), pl.ds(lo, hi - lo)), (pl.ds(lo, hi - lo), slice(None))
        copies = [
            pltpu.make_async_copy(src.at[at], dst.at[at], sems.at[3 * i + k])
            for k, (src, dst, at) in enumerate(
                ((momentum_ref, m_ref, lanes), (gradient_ref, g_ref, lanes), (basis_ref, b_ref, rows))
            )
        ]
        for copy in copies:
            copy.start()
        pieces.append((lo, hi, copies))
    left = None
    for lo, hi, copies in pieces:
        for copy in copies:
            copy.wait()
        blended = (m_ref[:, lo:hi].astype(F32) + g_ref[:, lo:hi].astype(F32)).astype(BF16)
        blended_ref[:, lo:hi] = blended
        part = jnp.dot(blended, b_ref[lo:hi, :], preferred_element_type=F32)
        left = part if left is None else left + part
    left_ref[...] = left.astype(BF16)


def blend(momentum, gradient, basis):
    rows, cols = momentum.shape
    rank = basis.shape[1]
    return pl.pallas_call(
        blend_body,
        out_shape=[held((rows, cols), BF16), held((rows, rank), BF16)],
        in_specs=[HBM] * 3,
        out_specs=[VMEM] * 2,
        scratch_shapes=[
            pltpu.VMEM((rows, cols), BF16),
            pltpu.VMEM((rows, cols), BF16),
            pltpu.VMEM((cols, rank), BF16),
            pltpu.SemaphoreType.DMA((9,)),
        ],
        compiler_params=pltpu.CompilerParams(vmem_limit_bytes=24 << 20),
        name="blend",
    )(*(pltpu.with_memory_space_constraint(a, pltpu.HBM) for a in (momentum, gradient, basis)))


def left_sum_body(parts_ref, out_ref):
    total = parts_ref[0].astype(F32)
    for i in range(1, parts_ref.shape[0]):
        total = total + parts_ref[i].astype(F32)
    low = total.astype(BF16)
    for i in range(out_ref.shape[0]):
        out_ref[i] = low


def project_body(blended_ref, left_ref, out_ref, work_ref):
    parts = out_ref.shape[0]
    rank = left_ref.shape[1]
    some = rank // parts
    block = blended_ref.shape[1] // parts
    left = left_ref[...]
    gram = split(lax.dot_general(left, left, ROWS_BY_ROWS, preferred_element_type=F32))[:TERMS]
    work_ref[...] = lax.dot_general(blended_ref[...], left, ROWS_BY_ROWS, preferred_element_type=F32)
    for f in range(parts):
        for i, term in enumerate(gram):
            out_ref[f, i * some : (i + 1) * some, :] = term[f * some : (f + 1) * some]
        out_ref[f, TERMS * some :, :] = work_ref[f * block : (f + 1) * block, :].astype(BF16)


def project_sum_body(parts_ref, out_ref, *, some):
    total = parts_ref[0].astype(F32)
    for i in range(1, parts_ref.shape[0]):
        total = total + parts_ref[i].astype(F32)
    high, low, _ = split(total[some : 2 * some] + total[:some])
    merged = jnp.concatenate([high, low, total[TERMS * some :].astype(BF16)], axis=0)
    for i in range(out_ref.shape[0]):
        out_ref[i] = merged


def diag_inverse(block):
    b = block.shape[0]
    n, width = b // 8, 2 * b
    eye = iota((b, b), 0) == iota((b, b), 1)
    aug = jnp.concatenate([block, jnp.where(eye, 1.0, 0.0)], axis=1)
    sub = iota((8, width), 0)
    rows = [aug[8 * i : 8 * i + 8] for i in range(n)]

    def spread(value, m):
        return jnp.broadcast_to(value[m : m + 1], (8, width))

    for g in range(n):
        cols = [
            [jnp.broadcast_to(rows[v][:, 8 * g + k : 8 * g + k + 1], (8, width)) for v in range(g, n)] for k in range(8)
        ]
        own, pivots, updates = rows[g], jnp.zeros((8, width), F32), []
        for m in range(0, 8, 2):
            first, second = cols[m], cols[m + 1]
            a, c, d = spread(first[0], m), spread(first[0], m + 1), spread(second[0], m + 1)
            det = a * d - c * c
            one_a, one_det = 1.0 / a, 1.0 / det
            pivots = jnp.where(sub == m, a, jnp.where(sub == m + 1, det * one_a, pivots))
            ia, ic, id_ = d * one_det, c * one_det, a * one_det
            below = sub > m + 1
            f0, f1 = jnp.where(below, first[0], 0.0), jnp.where(below, second[0], 0.0)

            def solved(value):
                x0, x1 = spread(value, m), spread(value, m + 1)
                return ia * x0 - ic * x1, id_ * x1 - ic * x0

            s0, s1 = solved(own)
            own = own - (f0 * s0 + f1 * s1) - jnp.where(sub == m + 1, c * one_a * spread(own, m), 0.0)
            updates += [(first[1:], s0), (second[1:], s1)]
            for k in range(m + 2, 8):
                t0, t1 = solved(cols[k][0])
                cols[k][0] = cols[k][0] - (f0 * t0 + f1 * t1)
                for v in range(1, n - g):
                    cols[k][v] = cols[k][v] - (first[v] * t0 + second[v] * t1)
        rows[g] = own * lax.rsqrt(pivots)
        for v in range(1, n - g):
            rows[g + v] = rows[g + v] - sum(col[v - 1] * s for col, s in updates)
    return jnp.concatenate(rows, axis=0)[:, b:]


def inverse_factor(gram, inv_ref):
    rank = gram.shape[0]
    row, col = iota((rank, rank), 0), iota((rank, rank), 1)
    inv_ref[...] = gram + jnp.where(row == col, 0.001, 0.0)
    lanes = iota((1, rank), 1)
    for p in range(0, rank, PANEL):
        q = p + PANEL
        inverse = diag_inverse(inv_ref[p:q, p:q])
        full = jnp.dot(left_terms(inverse, 1), right_terms(inv_ref[p:q, :]), preferred_element_type=F32)
        pieces = [full[:, :p]] if p else []
        pieces.append(inverse)
        if q < rank:
            pieces.append(full[:, q:])
        panel = jnp.concatenate(pieces, axis=1)
        inv_ref[p:q, :] = panel
        if q < rank:
            change = lax.dot_general(
                left_terms(panel[:, q:], 0), right_terms(panel), ROWS_BY_ROWS, preferred_element_type=F32
            )
            inv_ref[q:, :] = jnp.where((lanes >= p) & (lanes < q), 0.0, inv_ref[q:, :]) - change
    inv_ref[...] = jnp.where(row >= col, inv_ref[...], 0.0)


def by_inverse(low, inverse):
    terms = split(inverse)[:TERMS]
    return lax.dot_general(
        jnp.concatenate([low] * TERMS, axis=1), jnp.concatenate(terms, axis=1), COLS_BY_COLS, preferred_element_type=F32
    )


def product(a, b, dims, terms):
    if terms == 1:
        return lax.dot_general(a.astype(BF16), b.astype(BF16), dims, preferred_element_type=F32)
    (a_high, a_low, _), (b_high, b_low, _) = split(a), split(b)
    a = jnp.concatenate([a_high, a_high, a_low], axis=dims[0][0][0])
    b = jnp.concatenate([b_high, b_low, b_high], axis=dims[0][1][0])
    return lax.dot_general(a, b, dims, preferred_element_type=F32)


def refined_factor(gram, inv_ref):
    rank = gram.shape[0]
    row, col = iota((rank, rank), 0), iota((rank, rank), 1)
    eye = row == col
    gram = gram + jnp.where(eye, 0.001, 0.0)
    diag = jnp.where(eye, gram, 0.0)
    scale = lax.rsqrt(jnp.sum(diag, axis=0, keepdims=True))
    gram = gram * lax.rsqrt(jnp.sum(diag, axis=1, keepdims=True)) * scale
    inverse = jnp.where(eye, 1.0, jnp.where(row > col, -gram, 0.0))
    for terms in (1, 2, 2):
        error = product(product(inverse, gram, ROWS_BY_COLS, terms), inverse, COLS_BY_COLS, terms)
        error = error - jnp.where(eye, 1.0, 0.0)
        lower = jnp.where(row > col, error, jnp.where(eye, 0.5 * error, 0.0))
        inverse = inverse - product(lower, inverse, ROWS_BY_COLS, terms)
    inv_ref[...] = inverse * scale
    return jnp.sum(error * error)


def factor_body(parts_ref, inv_ref, proj_ref, colsq_ref):
    rank = inv_ref.shape[0]
    some = rank // parts_ref.shape[0]
    gram = parts_ref[:, :some, :].astype(F32) + parts_ref[:, some : 2 * some, :].astype(F32)
    gram = gram.reshape(rank, rank)
    proj_ref[...] = parts_ref[:, TERMS * some :, :].astype(F32).reshape(proj_ref.shape).astype(BF16)

    def spread_colsq():
        right = by_inverse(proj_ref[...], inv_ref[...])
        colsq = jnp.broadcast_to(jnp.sum(right * right, axis=0, keepdims=True), colsq_ref.shape[1:])
        for i in range(colsq_ref.shape[0]):
            colsq_ref[i] = colsq

    taken = refined_factor(gram, inv_ref)
    spread_colsq()

    @pl.when(jnp.logical_not(taken < 1e-4))
    def _():
        inverse_factor(gram, inv_ref)
        spread_colsq()


def feedback_body(blended_ref, left_ref, proj_ref, inv_ref, momentum_ref, ortho_ref):
    ortho_ref[...] = by_inverse(left_ref[...], inv_ref[...]).astype(BF16)
    right = by_inverse(proj_ref[...], inv_ref[...])
    feedback = lax.dot_general(ortho_ref[...], right.astype(BF16), COLS_BY_COLS, preferred_element_type=F32)
    momentum_ref[...] = (blended_ref[...].astype(F32) - 0.1 * feedback).astype(BF16)


def update_body(ortho_ref, proj_ref, inv_ref, colsq_ref, update_ref, basis_ref, product_ref, next_ref, sems):
    colsq = colsq_ref[0, 0:1, :]
    for i in range(1, colsq_ref.shape[0]):
        colsq = colsq + colsq_ref[i, 0:1, :]
    scale = lax.rsqrt(colsq + 1e-06)
    inverse, ortho, copies = inv_ref[...], ortho_ref[...], []
    for lo, hi in pieces_of(product_ref.shape[1], (0, 1, 3, 5, 8)):
        rows, lanes = (pl.ds(lo, hi - lo), slice(None)), (slice(None), pl.ds(lo, hi - lo))
        basis = (by_inverse(proj_ref[lo:hi, :], inverse) * scale).astype(BF16)
        next_ref[lo:hi, :] = basis
        copies.append(pltpu.make_async_copy(next_ref.at[rows], basis_ref.at[rows], sems.at[len(copies)]))
        copies[-1].start()
        product = lax.dot_general(ortho, basis, COLS_BY_COLS, preferred_element_type=F32)
        product_ref[:, lo:hi] = (SCALE * product).astype(BF16)
        copies.append(pltpu.make_async_copy(product_ref.at[lanes], update_ref.at[lanes], sems.at[len(copies)]))
        copies[-1].start()
    for copy in copies:
        copy.wait()


def on_device(momentum, gradient, basis, n_fsdp, n_tp):
    rank = basis.shape[1]
    rows, cols = momentum.shape
    some, block = rank // n_fsdp, cols // n_fsdp

    def exchange(parts, axis):
        if axis == "tp":
            return lax.all_to_all(parts, axis, 0, 0, tiled=True, axis_index_groups=[ORDERS[axis]])
        groups = [[n_tp * f + t for f in ORDERS[axis][t % 2]] for t in range(n_tp)]
        return lax.all_to_all(parts, ("fsdp", "tp"), 0, 0, tiled=True, axis_index_groups=groups)

    blended, left = blend(momentum, gradient, basis)
    parts = exchange(left.reshape(n_tp, rows // n_tp, rank), "tp")
    spread = call(left_sum_body, held(parts.shape, BF16), "left_sum", parts)
    left = exchange(spread, "tp").reshape(rows, rank)

    sent = held((n_fsdp, TERMS * some + block, rank), BF16)
    parts = call(project_body, sent, "project", blended, left, scratch=[pltpu.VMEM((cols, rank), F32)])
    merged = call(
        functools.partial(project_sum_body, some=some), held(parts.shape, BF16), "project_sum", exchange(parts, "fsdp")
    )
    inverse, proj, colsq = call(
        factor_body,
        [held((rank, rank)), held((cols, rank), BF16), held((n_tp, 8, rank))],
        "factor",
        exchange(merged, "fsdp"),
    )
    colsq = exchange(colsq, "tp")
    momentum_next, ortho = call(
        feedback_body,
        [shape((rows, cols), BF16), held((rows, rank), BF16)],
        "feedback",
        blended,
        left,
        proj,
        inverse,
    )
    update_next, basis_next = call(
        update_body,
        [pltpu.HBM((rows, cols), BF16), pltpu.HBM((cols, rank), BF16)],
        "update",
        ortho,
        proj,
        inverse,
        colsq,
        scratch=[pltpu.VMEM((rows, cols), BF16), pltpu.VMEM((cols, rank), BF16), pltpu.SemaphoreType.DMA((8,))],
        out_specs=[HBM, HBM],
    )
    return momentum_next, basis_next, update_next


def solution(mesh):
    body = functools.partial(on_device, n_fsdp=mesh.shape["fsdp"], n_tp=mesh.shape["tp"])
    return jax.shard_map(
        body,
        mesh=mesh,
        in_specs=(P("fsdp", "tp"), P("fsdp", "tp"), P("tp", None)),
        out_specs=(P("fsdp", "tp"), P("tp", None), P("fsdp", "tp")),
        check_vma=False,
    )
```
